768 devices in a mesh: rep: 8 (over y), seq: 24 (over z, core), fsdp: 4 (over x).
Axes of the slice: x: 4, y: 8, z: 12, core: 2. Of those that a mesh axis runs over, the one named last changes fastest.
Arguments:
- tokens: bfloat16 [49152, 4096], P(('rep', 'seq')), may hold values from -6 to 6
- cotangent: bfloat16 [49152, 4096], P(('rep', 'seq')), may hold values from -3 to 3
- norm_gain: float32 [4096], replicated, may hold values from 0.1 to 1.9
- gate_weight: bfloat16 [4096, 12288], P(None, ('seq', 'fsdp')), may hold values from -0.09375 to 0.09375
- up_weight: bfloat16 [4096, 12288], P(None, ('seq', 'fsdp')), may hold values from -0.09375 to 0.09375
- down_weight: bfloat16 [12288, 4096], P(('seq', 'fsdp')), may hold values from -0.0546875 to 0.0546875
- depths: int32 [49152], P(('rep', 'seq')), may hold values from 0 to 4, as said below
Outputs:
- branch_grad: bfloat16 [49152, 4096], P(('rep', 'seq', 'fsdp'))
- gate_grad: float32 [4096, 12288], P('rep', ('seq', 'fsdp'))
- up_grad: float32 [4096, 12288], P('rep', ('seq', 'fsdp'))
- down_grad: float32 [12288, 4096], P(('seq', 'fsdp'), 'rep')
The draws below stay inside these ranges and needn't reach their ends.
Inputs may be any that keep to these rules, and one draw needn't show every extreme that they name: `depths`: within each aligned block of 256 rows (the tokens of one seq shard) at most 8 and at least 4 tokens have a depth greater than 1, and some block has exactly 8.
All inputs are finite; a program needn't handle non-finite values.
Results may differ from the reference program's by a relative error of at most 0.019.
Values may be sent and summed in bfloat16 or wider, within the bound.
A program may use at most 64 MiB of HBM per device.

```python
from functools import partial
import jax
import jax.numpy as jnp
from jax import lax

D = 4096
FF = 12288
REC = 1
TOK_DEV = 256
MAXACT = 8
WINDOW = 6144
TOKENS = 49152
N_REP = 8


def draw_depths(key, part):
    shard_count = TOKENS // TOK_DEV
    counts = jax.random.randint(jax.random.fold_in(key, 102), (shard_count,), MAXACT // 2, MAXACT + 1, dtype=jnp.int32)
    busiest = jax.random.randint(jax.random.fold_in(key, 103), (), 0, shard_count, dtype=jnp.int32)
    counts = jnp.where(jnp.arange(shard_count, dtype=jnp.int32) == busiest, MAXACT, counts)
    scores = jax.random.randint(jax.random.fold_in(key, 104), (shard_count, TOK_DEV), 0, 1 << 20, dtype=jnp.int32)
    scores = scores * TOK_DEV + jnp.arange(TOK_DEV, dtype=jnp.int32)[None, :]
    ranking = jnp.argsort(jnp.argsort(scores, axis=1, stable=True), axis=1, stable=True).astype(jnp.int32)
    chosen = ranking < counts[:, None]
    deeper = jax.random.randint(jax.random.fold_in(key, 105), (shard_count, TOK_DEV), REC + 1, 5, dtype=jnp.int32)
    shallow = jax.random.randint(jax.random.fold_in(key, 106), (shard_count, TOK_DEV), 0, REC + 1, dtype=jnp.int32)
    return jnp.where(chosen, deeper, shallow).reshape(TOKENS)


def block_levels(stream_key, dims, shards, low, high):
    level, own = 1.0, jax.random.fold_in(stream_key, 6)
    for dim, parts in shards:
        steps = jnp.exp(jax.random.uniform(jax.random.fold_in(own, dim), (parts,), jnp.float32, low / len(shards), high / len(shards)))
        level = level * jnp.repeat(steps, dims[dim] // parts).reshape([-1 if axis == dim else 1 for axis in range(len(dims))])
    return level


def noise(rng, extent, scale, bound, shards=(), held_as=jnp.bfloat16):
    level = block_levels(rng, extent, shards, -0.22, 0.18) if shards else 1.0
    entries = jax.random.normal(rng, extent, jnp.float32) * scale * level
    return jnp.minimum(jnp.maximum(entries, -bound), bound).astype(held_as)


def setup_inputs(seed: int = 0) -> dict:
    seeds = jax.random.split(jax.random.key(seed), 8)
    tokens = noise(seeds[0], (TOKENS, D), 1.0, 6.0, ((0, 192),))
    cotangent = noise(seeds[1], (TOKENS, D), 0.5, 3.0, ((0, 192),))
    norm_gain = jnp.clip(1.0 + 0.18 * jax.random.normal(seeds[2], (D,), jnp.float32), 0.1, 1.9)
    gate_weight = noise(seeds[3], (D, FF), D ** -0.5, 0.09375, ((1, 96),))
    up_weight = noise(seeds[4], (D, FF), D ** -0.5, 0.09375, ((1, 96),))
    down_weight = noise(seeds[5], (FF, D), FF ** -0.5, 0.0546875, ((0, 96),))
    depths = draw_depths(jax.random.fold_in(seeds[7], 71), 0)
    return dict(tokens=tokens, cotangent=cotangent, norm_gain=norm_gain, gate_weight=gate_weight, up_weight=up_weight, down_weight=down_weight, depths=depths)


EPSILON = 1e-05

def normalize(widened, norm_gain):
    factor = lax.rsqrt(lax.optimization_barrier(jnp.mean(widened * widened, axis=-1, keepdims=True)) + EPSILON)
    return widened * factor * norm_gain

def rounded(term):
    narrow = lax.optimization_barrier(term.astype(jnp.bfloat16))
    return narrow.astype(jnp.float32)

def reference(tokens, cotangent, norm_gain, gate_weight, up_weight, down_weight, depths):
    active = depths > REC
    widened = tokens.astype(jnp.float32)
    normed = normalize(widened, norm_gain).astype(jnp.bfloat16)
    masked = jnp.where(active[:, None], cotangent, jnp.zeros_like(cotangent))
    gate = jnp.dot(normed, gate_weight, preferred_element_type=jnp.float32)
    up = jnp.dot(normed, up_weight, preferred_element_type=jnp.float32)
    sigmoid_gate = jax.nn.sigmoid(gate)
    swished = gate * sigmoid_gate
    hidden = (swished * up).astype(jnp.bfloat16)
    hidden_grad = jnp.dot(masked, down_weight.T, preferred_element_type=jnp.float32)
    gate_rows = (hidden_grad * up * sigmoid_gate * (1.0 + gate * (1.0 - sigmoid_gate))).astype(jnp.bfloat16)
    up_rows = (hidden_grad * swished).astype(jnp.bfloat16)

    def replica_terms(carry, pieces):
        normed_part, masked_part, hidden_part, gate_part, up_part = pieces
        gate_term = jnp.dot(normed_part.T, gate_part, preferred_element_type=jnp.float32)
        up_term = jnp.dot(normed_part.T, up_part, preferred_element_type=jnp.float32)
        down_term = jnp.dot(hidden_part.T, masked_part, preferred_element_type=jnp.float32)
        return ((carry[0] + rounded(gate_term), carry[1] + rounded(up_term), carry[2] + rounded(down_term)), None)
    pieces = (normed.reshape(N_REP, WINDOW, D), masked.reshape(N_REP, WINDOW, D), hidden.reshape(N_REP, WINDOW, FF), gate_rows.reshape(N_REP, WINDOW, FF), up_rows.reshape(N_REP, WINDOW, FF))
    initial = (jnp.zeros((D, FF), jnp.float32), jnp.zeros((D, FF), jnp.float32), jnp.zeros((FF, D), jnp.float32))
    grads, _ = lax.scan(replica_terms, initial, pieces)
    feature_grad = jnp.dot(gate_rows, gate_weight.T, preferred_element_type=jnp.float32)
    feature_grad = feature_grad + jnp.dot(up_rows, up_weight.T, preferred_element_type=jnp.float32)
    _, pullback = jax.vjp(partial(normalize, norm_gain=norm_gain), widened)
    branch_grad = pullback(feature_grad)[0].astype(jnp.bfloat16)
    return (branch_grad, grads[0], grads[1], grads[2])
```

```python
import functools

import jax
import jax.numpy as jnp
from jax import lax
from jax.experimental import pallas as pl
from jax.experimental.pallas import tpu as pltpu
from jax.sharding import PartitionSpec as P

REC = 1
SLOTS = 8
EPSILON = 1e-05
MESH = pl.DeviceIdType.MESH
BF = jnp.bfloat16
F32 = jnp.float32


def dot(a, b, da=1, db=0):
    return lax.dot_general(a, b, (((da,), (db,)), ((), ())), preferred_element_type=F32)


def remote(src, dst, ssem, rsem, device):
    return pltpu.make_async_remote_copy(
        src_ref=src,
        dst_ref=dst,
        send_sem=ssem,
        recv_sem=rsem,
        device_id=device,
        device_id_type=MESH,
    )


class PlaneGather:
    def __init__(self, buf, sems, where, sizes, device, sent):
        self.buf, self.sent, self.device = buf, sent, device
        self.zs, self.zr, self.xs, self.xr, self.cs, self.cr = sems
        self.y, self.z, self.c, self.x = where
        self.Y, self.Z, self.X = sizes
        self.p = lax.rem(self.x, 2)
        self.right, self.left = self.Z // 2, (self.Z - 1) // 2
        self.here = device(self.y, self.z, self.c, self.x)

    def zz(self, way, s):
        return lax.rem(self.z + (self.Z - s if way == 0 else s), self.Z)

    def go(self, copy):
        copy.start()
        self.sent.append(copy)

    def forward(self, way, s, block):
        step = 1 if way == 0 else self.Z - 1
        to = self.device(self.y, lax.rem(self.z + step, self.Z), self.c, self.x)
        part = self.buf.at[block, self.c, self.p]
        self.go(remote(part, part, self.zs.at[way, s], self.zr.at[way, s], to))

    def to_core(self, part, way, s, kind):
        to = self.device(self.y, self.z, 1 - self.c, self.x)
        self.go(remote(part, part, self.cs.at[way, s, kind], self.cr.at[way, s, kind], to))

    def start(self):
        self.forward(0, 1, self.z)
        if self.left:
            self.forward(1, 1, self.z)
        self.to_core(self.buf.at[self.z, self.c], 0, 0, 0)

    def arrive_one(self, way, s, last):
        block = self.zz(way, s)
        part = self.buf.at[block, self.c, self.p]
        remote(part, part, self.zs.at[way, s], self.zr.at[way, s], self.here).wait_recv()
        if s < last:
            self.forward(way, s + 1, block)
        for q in range(2):
            xx = lax.rem(self.x + (1 if q == 0 else self.X - 1), self.X)
            to = self.device(self.y, self.z, self.c, xx)
            quarter = self.buf.at[block, self.c, self.p, q]
            self.go(remote(quarter, quarter, self.xs.at[way, s, q], self.xr.at[way, s, q], to))
        self.to_core(part, way, s, 0)

    def beside_one(self, way, s):
        block = self.zz(way, s)
        for q in range(2):
            quarter = self.buf.at[block, self.c, 1 - self.p, q]
            remote(
                quarter, quarter, self.xs.at[way, s, q], self.xr.at[way, s, q], self.here
            ).wait_recv()
        self.to_core(self.buf.at[block, self.c, 1 - self.p], way, s, 1)

    def arrive(self, s):
        if 1 <= s <= self.right:
            self.arrive_one(0, s, self.right)
        if 1 <= s <= self.left:
            self.arrive_one(1, s, self.left)
        if 1 <= s - 1 <= self.right:
            self.beside_one(0, s - 1)
        if 1 <= s - 1 <= self.left:
            self.beside_one(1, s - 1)

    def finish(self):
        part = self.buf.at[self.z, 1 - self.c]
        remote(part, part, self.cs.at[0, 0, 0], self.cr.at[0, 0, 0], self.here).wait_recv()
        for way, last in ((0, self.right), (1, self.left)):
            for s in range(1, last + 1):
                block = self.zz(way, s)
                for kind in range(2):
                    h = self.p if kind == 0 else 1 - self.p
                    part = self.buf.at[block, 1 - self.c, h]
                    remote(
                        part, part, self.cs.at[way, s, kind], self.cr.at[way, s, kind], self.here
                    ).wait_recv()


def kernel(
    sizes,
    tok_hbm,
    cot_hbm,
    gain_ref,
    gw_hbm,
    uw_hbm,
    dw_hbm,
    dep_ref,
    out_b,
    out_g,
    out_u,
    out_d,
    tok,
    cot,
    wgu,
    dw,
    source,
    picks,
    G,
    H,
    S,
    R,
    FAs,
    FAr,
    FO,
    FBs,
    FBr,
    FT,
    FCs,
    FCr,
    FDr,
    lsem,
    gsems,
    hsems,
    asems,
    ysems,
    fsems,
):
    Y, Z, X = sizes
    n_tok, D = tok.shape
    ff = dw.shape[0]
    N = Z * 2 * SLOTS
    QD, HD, CW = D // 4, D // (4 * Y), D // (2 * X)
    y, x = lax.axis_index("rep"), lax.axis_index("fsdp")
    seq = lax.axis_index("seq")
    z, c = seq // 2, lax.rem(seq, 2)

    def device(yy, zz, cc, xx):
        return (yy, zz * 2 + cc, xx)

    loads = [
        pltpu.make_async_copy(tok_hbm, tok, lsem.at[0]),
        pltpu.make_async_copy(cot_hbm, cot, lsem.at[1]),
        pltpu.make_async_copy(gw_hbm, wgu.at[:, 0:ff], lsem.at[2]),
        pltpu.make_async_copy(uw_hbm, wgu.at[:, ff : 2 * ff], lsem.at[3]),
        pltpu.make_async_copy(dw_hbm, dw, lsem.at[4]),
    ]
    for load in loads:
        load.start()

    partners = [device(lax.rem(y + d, Y), z, c, x) for d in range(1, Y)]
    partners += [device(y, lax.rem(z + d, Z), c, x) for d in range(1, Z)]
    mine = c * X + x

    def corner(d):
        j = lax.rem(mine + d, 2 * X)
        return device(y, z, j // X, lax.rem(j, X))

    partners += [corner(d) for d in range(1, 2 * X)]
    barrier = pltpu.get_barrier_semaphore()
    for partner in partners:
        pl.semaphore_signal(barrier, inc=1, device_id=partner, device_id_type=MESH)

    act = jnp.where(dep_ref[...] > REC, 1.0, 0.0).astype(F32)
    act = jnp.broadcast_to(act, (16, n_tok))
    before = lax.broadcasted_iota(jnp.int32, (n_tok, n_tok), 0)
    after = lax.broadcasted_iota(jnp.int32, (n_tok, n_tok), 1)
    tri = jnp.where(before <= after, 1.0, 0.0).astype(BF)
    ordinal = dot(act.astype(BF), tri) - 1.0
    slot = lax.broadcasted_iota(jnp.int32, (16, n_tok), 0).astype(F32)
    sel = jnp.where((ordinal == slot) & (act > 0.5), 1.0, 0.0).astype(BF)
    own = n_tok // X
    i0 = lax.broadcasted_iota(jnp.int32, (own, n_tok), 0)
    i1 = lax.broadcasted_iota(jnp.int32, (own, n_tok), 1)
    rows = jnp.where(i1 == i0 + x * own, 1.0, 0.0).astype(BF)
    picks[...] = dot(rows, sel, 1, 1).astype(BF)
    loads[0].wait()
    tsel = dot(sel, tok[...])
    factor = lax.rsqrt(jnp.mean(tsel * tsel, axis=-1, keepdims=True) + EPSILON)
    normed = tsel * factor * gain_ref[...]
    source[...] = tsel[:SLOTS]
    loads[1].wait()
    csel = dot(sel, cot[...])
    block = jnp.concatenate([normed[:SLOTS], csel[:SLOTS]], axis=0).astype(BF)
    for h in range(2):
        for q in range(2):
            at = (h * 2 + q) * QD
            G[z, c, h, q] = block[:, at : at + QD]
    for yy in range(Y):
        for h in range(2):
            for q in range(2):
                at = (yy * 4 + h * 2 + q) * HD
                S[yy, h, q] = block[:, at : at + HD]
    for h in range(2):
        for q in range(2):
            H[z, c, h, q, y] = S[y, h, q]

    pl.semaphore_wait(barrier, len(partners))

    sent = []

    def go(copy):
        copy.start()
        sent.append(copy)

    where = (y, z, c, x)
    gather = PlaneGather(G, gsems, where, sizes, device, sent)
    gather.start()
    as_, ar = asems
    for d in range(1, Y):
        yy = lax.rem(y + d, Y)
        go(
            remote(
                S.at[yy], H.at[z, c, :, :, y], as_.at[d], ar.at[d], device(yy, z, c, x)
            )
        )
    for s in range(1, gather.right + 1):
        gather.arrive(s)
    gather.arrive(gather.right + 1)
    for d in range(1, Y):
        yy = lax.rem(y + Y - d, Y)
        part = H.at[z, c, :, :, yy]
        remote(S.at[yy], part, as_.at[d], ar.at[d], device(y, z, c, x)).wait_recv()
    wide = PlaneGather(H, hsems, where, sizes, device, sent)
    wide.start()
    gather.finish()

    for load in loads[2:]:
        load.wait()
    gu = jnp.zeros((2 * N, 2 * ff), F32)
    hd = jnp.zeros((2 * N, ff), F32)
    for h in range(2):
        for q in range(2):
            at = (h * 2 + q) * QD
            a = G[:, :, h, q].reshape(2 * N, QD)
            gu += dot(a, wgu[at : at + QD, :])
            hd += dot(a, dw[:, at : at + QD], 1, 1)
    gu = gu.reshape(Z * 2, 2, SLOTS, 2 * ff)[:, 0].reshape(N, 2 * ff)
    hg = hd.reshape(Z * 2, 2, SLOTS, ff)[:, 1].reshape(N, ff)
    gate, up = gu[:, :ff], gu[:, ff:]
    sig = jax.nn.sigmoid(gate)
    swished = gate * sig
    hidden = (swished * up).astype(BF)
    gate_rows = (hg * up * sig * (1.0 + gate * (1.0 - sig))).astype(BF)
    up_rows = (hg * swished).astype(BF)
    for k in range(2):
        half = slice(k * N // 2, (k + 1) * N // 2)
        R[y, k, 0] = gate_rows[half]
        R[y, k, 1] = up_rows[half]
        R[y, k, 2] = hidden[half]

    ys, yr = ysems

    def y_forward(way, k, unit):
        step = 1 if way == 0 else Y - 1
        to = device(lax.rem(y + step, Y), z, c, x)
        part = R.at[unit] if k < Y // 2 else R.at[unit, way]
        go(remote(part, part, ys.at[way, k], yr.at[way, k], to))

    def y_arrive(k):
        for way in range(2):
            unit = lax.rem(y + (Y - k if way == 0 else k), Y)
            part = R.at[unit] if k < Y // 2 else R.at[unit, way]
            remote(part, part, ys.at[way, k], yr.at[way, k], device(y, z, c, x)).wait_recv()
            if k < Y // 2:
                y_forward(way, k + 1, unit)

    for way in range(2):
        y_forward(way, 1, y)

    wide.arrive(1)

    f_as, f_ar, f_bs, f_br, f_cs, f_cr, f_ds, f_dr = fsems
    both = jnp.concatenate([gate_rows, up_rows], axis=1)
    other = device(y, z, 1 - c, x)
    for d in range(X):
        at = pl.multiple_of(((1 - c) * X + d) * CW, CW)
        FAs[d] = dot(both, wgu[pl.ds(at, CW), :], 1, 1).astype(BF)
        go(remote(FAs.at[d], FAr.at[d], f_as.at[d], f_ar.at[d], other))
    wide.arrive(2)
    for d in range(X):
        at = pl.multiple_of((c * X + d) * CW, CW)
        FO[d] = dot(both, wgu[pl.ds(at, CW), :], 1, 1)
    wide.arrive(3)
    for d in range(X):
        remote(FAs.at[d], FAr.at[d], f_as.at[d], f_ar.at[d], other).wait_recv()
    for d in range(1, X):
        xx = lax.rem(x + d, X)
        FBs[d] = (FO[xx] + FAr[xx].astype(F32)).astype(BF)
        go(remote(FBs.at[d], FBr.at[d], f_bs.at[d], f_br.at[d], device(y, z, c, xx)))
    for s in range(4, gather.right + 2):
        wide.arrive(s)
    total = FO[x] + FAr[x].astype(F32)
    for d in range(1, X):
        remote(FBs.at[d], FBr.at[d], f_bs.at[d], f_br.at[d], other).wait_recv()
        total += FBr[d].astype(F32)
    FT[...] = total.reshape(Z, 16, CW)
    FCs[...] = total.astype(BF).reshape(Z, 16, CW)
    for d in range(1, Z):
        zz = lax.rem(z + d, Z)
        go(remote(FCs.at[zz], FCr.at[d], f_cs.at[d], f_cr.at[d], device(y, zz, c, x)))
    if Y > 2:
        y_arrive(1)
    total = FT[z]
    for d in range(1, Z):
        remote(FCs.at[z], FCr.at[d], f_cs.at[d], f_cr.at[d], other).wait_recv()
        total += FCr[d].astype(F32)
    FDr[mine] = total.astype(BF)
    for d in range(1, 2 * X):
        go(remote(FDr.at[mine], FDr.at[mine], f_ds.at[d], f_dr.at[d], corner(d)))
    wide.finish()

    def accumulate(unit, first):
        rows_g = jnp.concatenate([R[unit, 0, 0], R[unit, 1, 0]], axis=0)
        rows_u = jnp.concatenate([R[unit, 0, 1], R[unit, 1, 1]], axis=0)
        rows_h = jnp.concatenate([R[unit, 0, 2], R[unit, 1, 2]], axis=0)
        gu_rows = jnp.concatenate([rows_g, rows_u], axis=1)
        for h in range(2):
            for q in range(2):
                at = (h * 2 + q) * HD
                a = H[:, :, h, q, unit].astype(F32).reshape(Z * 2, 2, SLOTS, HD)
                nrm = a[:, 0].reshape(N, HD).astype(BF)
                msk = a[:, 1].reshape(N, HD).astype(BF)
                pair = dot(nrm, gu_rows, 0, 0)
                down = dot(rows_h, msk, 0, 0)
                if first:
                    out_g[at : at + HD, :] = pair[:, :ff]
                    out_u[at : at + HD, :] = pair[:, ff:]
                    out_d[:, at : at + HD] = down
                else:
                    out_g[at : at + HD, :] += pair[:, :ff]
                    out_u[at : at + HD, :] += pair[:, ff:]
                    out_d[:, at : at + HD] += down

    def accumulate_pair(k):
        accumulate(lax.rem(y + Y - k, Y), False)
        if k < Y // 2:
            accumulate(lax.rem(y + k, Y), False)

    accumulate(y, True)
    done = 1
    for k in range(2, Y // 2):
        y_arrive(k)
        accumulate_pair(done)
        done = k

    for d in range(1, 2 * X):
        j = lax.rem(mine + 2 * X - d, 2 * X)
        remote(FDr.at[j], FDr.at[j], f_ds.at[d], f_dr.at[d], other).wait_recv()
    pieces = []
    for j in range(2 * X):
        piece = FDr[j].astype(F32)
        pieces.append(jnp.where(c == 0, piece[:SLOTS], piece[SLOTS:]))
    feature = jnp.concatenate(pieces, axis=1)
    src = source[...]
    scale = lax.rsqrt(jnp.mean(src * src, axis=-1, keepdims=True) + EPSILON)
    weighted = feature * gain_ref[...]
    along = jnp.mean(weighted * src, axis=-1, keepdims=True)
    grad = weighted * scale - src * (scale * scale * scale * along)
    grad = jnp.concatenate([grad, jnp.zeros_like(grad)], axis=0).astype(BF)
    out_b[...] = dot(picks[...], grad).astype(BF)

    while done < Y // 2 - 1:
        done += 1
        accumulate_pair(done - 1)
    if Y > 2:
        accumulate_pair(done)
    y_arrive(Y // 2)
    accumulate_pair(Y // 2)
    for copy in sent:
        copy.wait_send()


def local(sizes, tokens, cotangent, norm_gain, gate_weight, up_weight, down_weight, depths):
    Y, Z, X = sizes
    n_tok, D = tokens.shape
    ff = gate_weight.shape[1]
    N = Z * 2 * SLOTS
    QD, HD, CW = D // 4, D // (4 * Y), D // (2 * X)
    vmem, dma = pltpu.VMEM, pltpu.SemaphoreType.DMA
    steps = Z // 2 + 1
    plane = (
        dma((2, steps)),
        dma((2, steps)),
        dma((2, steps, 2)),
        dma((2, steps, 2)),
        dma((2, steps, 2)),
        dma((2, steps, 2)),
    )
    hbm, whole = pl.BlockSpec(memory_space=pl.ANY), pl.BlockSpec(memory_space=pltpu.VMEM)
    return pl.pallas_call(
        functools.partial(kernel, sizes),
        out_shape=(
            jax.ShapeDtypeStruct((n_tok // X, D), BF),
            jax.ShapeDtypeStruct((D // Y, ff), F32),
            jax.ShapeDtypeStruct((D // Y, ff), F32),
            jax.ShapeDtypeStruct((ff, D // Y), F32),
        ),
        in_specs=[hbm, hbm, whole, hbm, hbm, hbm, whole],
        out_specs=(whole,) * 4,
        scratch_shapes=[
            vmem((n_tok, D), BF),
            vmem((n_tok, D), BF),
            vmem((D, 2 * ff), BF),
            vmem((ff, D), BF),
            vmem((SLOTS, D), F32),
            vmem((n_tok // X, 16), BF),
            vmem((Z, 2, 2, 2, 16, QD), BF),
            vmem((Z, 2, 2, 2, Y, 16, HD), BF),
            vmem((Y, 2, 2, 16, HD), BF),
            vmem((Y, 2, 3, N // 2, ff), BF),
            vmem((X, N, CW), BF),
            vmem((X, N, CW), BF),
            vmem((X, N, CW), F32),
            vmem((X, N, CW), BF),
            vmem((X, N, CW), BF),
            vmem((Z, 16, CW), F32),
            vmem((Z, 16, CW), BF),
            vmem((Z, 16, CW), BF),
            vmem((2 * X, 16, CW), BF),
            dma((5,)),
            plane,
            plane,
            (dma((Y,)), dma((Y,))),
            (dma((2, Y // 2 + 1)), dma((2, Y // 2 + 1))),
            (
                dma((X,)),
                dma((X,)),
                dma((X,)),
                dma((X,)),
                dma((Z,)),
                dma((Z,)),
                dma((2 * X,)),
                dma((2 * X,)),
            ),
        ],
        compiler_params=pltpu.CompilerParams(
            collective_id=0, has_side_effects=True, vmem_limit_bytes=58 * 1024 * 1024
        ),
    )(
        tokens,
        cotangent,
        norm_gain.reshape(1, D),
        gate_weight,
        up_weight,
        down_weight,
        depths.reshape(1, n_tok),
    )


def solution(mesh):
    sizes = (mesh.shape["rep"], mesh.shape["seq"] // 2, mesh.shape["fsdp"])
    rows, hidden = ("rep", "seq"), ("seq", "fsdp")
    return jax.shard_map(
        functools.partial(local, sizes),
        mesh=mesh,
        in_specs=(
            P(rows, None),
            P(rows, None),
            P(),
            P(None, hidden),
            P(None, hidden),
            P(hidden, None),
            P(rows),
        ),
        out_specs=(
            P(("rep", "seq", "fsdp"), None),
            P("rep", hidden),
            P("rep", hidden),
            P(hidden, "rep"),
        ),
        check_vma=False,
    )
```

```python
import functools

import jax
import jax.numpy as jnp
from jax import lax
from jax.experimental import pallas as pl
from jax.experimental.pallas import tpu as pltpu
from jax.sharding import PartitionSpec as P

REC = 1
SLOTS = 8
EPSILON = 1e-05
MESH = pl.DeviceIdType.MESH
BF = jnp.bfloat16
F32 = jnp.float32


def dot(a, b, da=1, db=0):
    return lax.dot_general(a, b, (((da,), (db,)), ((), ())), preferred_element_type=F32)


def remote(src, dst, ssem, rsem, device):
    return pltpu.make_async_remote_copy(
        src_ref=src,
        dst_ref=dst,
        send_sem=ssem,
        recv_sem=rsem,
        device_id=device,
        device_id_type=MESH,
    )


def tree(half):
    return [[s for s in (g + 2, g + 1) if s <= half] for g in range(0, half, 2)]


def farthest_first(n):
    return sorted(range(n), key=lambda d: -min(d, n - d))


class PlaneGather:
    def __init__(self, buf, sems, where, sizes, device, sent):
        self.buf, self.sent, self.device = buf, sent, device
        self.zs, self.zr, self.xs, self.xr, self.cs, self.cr = sems
        self.y, self.z, self.c, self.x = where
        self.Y, self.Z, self.X = sizes
        self.p = lax.rem(self.x, 2)
        self.half = self.Z // 2
        self.here = device(self.y, self.z, self.c, self.x)
        self.groups = tree(self.half)

    def events(self):
        found = []
        for k, group in enumerate(self.groups):
            found.append(functools.partial(self.arrive, group[0]))
            if k:
                found += [functools.partial(self.beside, s) for s in self.groups[k - 1]]
            found += [functools.partial(self.arrive, s) for s in group[1:]]
        return found + [functools.partial(self.beside, s) for s in self.groups[-1]]

    def zz(self, way, s):
        return lax.rem(self.z + (self.Z - s if way == 0 else s), self.Z)

    def go(self, copy):
        copy.start()
        self.sent.append(copy)

    def quarters(self, way, s):
        return (0, 1) if s < self.half else (way,)

    def part(self, way, s, block, c, h):
        whole = self.buf.at[block, c, h]
        return whole if s < self.half else self.buf.at[block, c, h, way]

    def forward(self, held, block):
        for s in (held + 2, held + 1):
            if s <= self.half:
                for way in range(2):
                    step = s - held if way == 0 else self.Z - (s - held)
                    to = self.device(self.y, lax.rem(self.z + step, self.Z), self.c, self.x)
                    part = self.part(way, s, block[way], self.c, self.p)
                    self.go(remote(part, part, self.zs.at[way, s], self.zr.at[way, s], to))

    def to_core(self, part, way, s, kind):
        to = self.device(self.y, self.z, 1 - self.c, self.x)
        self.go(remote(part, part, self.cs.at[way, s, kind], self.cr.at[way, s, kind], to))

    def start(self):
        self.forward(0, (self.z, self.z))
        self.to_core(self.buf.at[self.z, self.c], 0, 0, 0)

    def arrive(self, s):
        blocks = (self.zz(0, s), self.zz(1, s))
        parts = [self.part(way, s, blocks[way], self.c, self.p) for way in range(2)]
        for way in range(2):
            remote(
                parts[way], parts[way], self.zs.at[way, s], self.zr.at[way, s], self.here
            ).wait_recv()
        if s % 2 == 0:
            self.forward(s, blocks)
        for way in range(2):
            for q in self.quarters(way, s):
                xx = lax.rem(self.x + (1 if q == 0 else self.X - 1), self.X)
                to = self.device(self.y, self.z, self.c, xx)
                quarter = self.buf.at[blocks[way], self.c, self.p, q]
                self.go(
                    remote(quarter, quarter, self.xs.at[way, s, q], self.xr.at[way, s, q], to)
                )
            self.to_core(parts[way], way, s, 0)

    def beside(self, s):
        for way in range(2):
            block = self.zz(way, s)
            for q in self.quarters(way, s):
                quarter = self.buf.at[block, self.c, 1 - self.p, q]
                remote(
                    quarter, quarter, self.xs.at[way, s, q], self.xr.at[way, s, q], self.here
                ).wait_recv()
            self.to_core(self.part(way, s, block, self.c, 1 - self.p), way, s, 1)

    def finish(self):
        part = self.buf.at[self.z, 1 - self.c]
        remote(part, part, self.cs.at[0, 0, 0], self.cr.at[0, 0, 0], self.here).wait_recv()
        for s in range(1, self.half + 1):
            for way in range(2):
                block = self.zz(way, s)
                for kind in range(2):
                    h = self.p if kind == 0 else 1 - self.p
                    part = self.part(way, s, block, 1 - self.c, h)
                    remote(
                        part, part, self.cs.at[way, s, kind], self.cr.at[way, s, kind], self.here
                    ).wait_recv()


def kernel(
    sizes,
    tok_hbm,
    cot_hbm,
    gain_ref,
    gw_hbm,
    uw_hbm,
    dw_hbm,
    dep_ref,
    out_s,
    out_p,
    out_g,
    out_u,
    out_d,
    tok,
    cot,
    wgu,
    dw,
    source,
    G,
    H,
    S,
    R,
    FAs,
    FAr,
    B,
    FBs,
    FBr,
    FT,
    FCs,
    FCr,
    FDr,
    lsem,
    gsems,
    hsems,
    asems,
    ysems,
    fsems,
):
    Y, Z, X = sizes
    n_tok, D = tok.shape
    ff = dw.shape[0]
    N = Z * 2 * SLOTS
    QD, HD, CW = D // 4, D // (4 * Y), D // (2 * X)
    y, x = lax.axis_index("rep"), lax.axis_index("fsdp")
    seq = lax.axis_index("seq")
    z, c = seq // 2, lax.rem(seq, 2)

    def device(yy, zz, cc, xx):
        return (yy, zz * 2 + cc, xx)

    loads = [
        pltpu.make_async_copy(tok_hbm, tok, lsem.at[0]),
        pltpu.make_async_copy(cot_hbm, cot, lsem.at[1]),
        pltpu.make_async_copy(gw_hbm, wgu.at[:, 0:ff], lsem.at[2]),
        pltpu.make_async_copy(uw_hbm, wgu.at[:, ff : 2 * ff], lsem.at[3]),
        pltpu.make_async_copy(dw_hbm, dw, lsem.at[4]),
    ]
    for load in loads:
        load.start()

    partners = [device(lax.rem(y + d, Y), z, c, x) for d in range(1, Y)]
    partners += [device(y, lax.rem(z + d, Z), c, x) for d in range(1, Z)]
    mine = c * X + x

    def corner(d):
        j = lax.rem(mine + d, 2 * X)
        return device(y, z, j // X, lax.rem(j, X))

    partners += [corner(d) for d in range(1, 2 * X)]
    barrier = pltpu.get_barrier_semaphore()
    for partner in partners:
        pl.semaphore_signal(barrier, inc=1, device_id=partner, device_id_type=MESH)

    act = jnp.where(dep_ref[...] > REC, 1.0, 0.0).astype(F32)
    act = jnp.broadcast_to(act, (16, n_tok))
    before = lax.broadcasted_iota(jnp.int32, (n_tok, n_tok), 0)
    after = lax.broadcasted_iota(jnp.int32, (n_tok, n_tok), 1)
    tri = jnp.where(before <= after, 1.0, 0.0).astype(BF)
    ordinal = dot(act.astype(BF), tri) - 1.0
    slot = lax.broadcasted_iota(jnp.int32, (16, n_tok), 0).astype(F32)
    sel = jnp.where((ordinal == slot) & (act > 0.5), 1.0, 0.0).astype(BF)
    own = n_tok // X
    i0 = lax.broadcasted_iota(jnp.int32, (own, n_tok), 0)
    i1 = lax.broadcasted_iota(jnp.int32, (own, n_tok), 1)
    rows = jnp.where(i1 == i0 + x * own, 1.0, 0.0).astype(BF)
    out_p[...] = dot(rows, sel, 1, 1).astype(BF)
    loads[0].wait()
    tsel = dot(sel, tok[...])
    factor = lax.rsqrt(jnp.mean(tsel * tsel, axis=-1, keepdims=True) + EPSILON)
    normed = tsel * factor * gain_ref[...]
    source[...] = tsel[:SLOTS]
    loads[1].wait()
    csel = dot(sel, cot[...])
    block = jnp.concatenate([normed[:SLOTS], csel[:SLOTS]], axis=0).astype(BF)
    for h in range(2):
        for q in range(2):
            at = (h * 2 + q) * QD
            G[z, c, h, q] = block[:, at : at + QD]
    for yy in range(Y):
        for h in range(2):
            for q in range(2):
                at = (yy * 4 + h * 2 + q) * HD
                S[yy, h, q] = block[:, at : at + HD]
    for h in range(2):
        for q in range(2):
            H[z, c, h, q, y] = S[y, h, q]

    pl.semaphore_wait(barrier, len(partners))

    sent = []

    def go(copy):
        copy.start()
        sent.append(copy)

    where = (y, z, c, x)
    gather = PlaneGather(G, gsems, where, sizes, device, sent)
    gather.start()
    as_, ar = asems
    for d in range(1, Y):
        yy = lax.rem(y + d, Y)
        go(
            remote(
                S.at[yy], H.at[z, c, :, :, y], as_.at[d], ar.at[d], device(yy, z, c, x)
            )
        )
    for event in gather.events():
        event()
    for d in range(1, Y):
        yy = lax.rem(y + Y - d, Y)
        part = H.at[z, c, :, :, yy]
        remote(S.at[yy], part, as_.at[d], ar.at[d], device(y, z, c, x)).wait_recv()
    wide = PlaneGather(H, hsems, where, sizes, device, sent)
    wide.start()
    gather.finish()

    for load in loads[2:]:
        load.wait()
    gu = jnp.zeros((2 * N, 2 * ff), F32)
    hd = jnp.zeros((2 * N, ff), F32)
    for h in range(2):
        for q in range(2):
            at = (h * 2 + q) * QD
            a = G[:, :, h, q].reshape(2 * N, QD)
            gu += dot(a, wgu[at : at + QD, :])
            hd += dot(a, dw[:, at : at + QD], 1, 1)
    gu = gu.reshape(Z * 2, 2, SLOTS, 2 * ff)[:, 0].reshape(N, 2 * ff)
    hg = hd.reshape(Z * 2, 2, SLOTS, ff)[:, 1].reshape(N, ff)
    gate, up = gu[:, :ff], gu[:, ff:]
    sig = jax.nn.sigmoid(gate)
    swished = gate * sig
    hidden = (swished * up).astype(BF)
    gate_rows = (hg * up * sig * (1.0 + gate * (1.0 - sig))).astype(BF)
    up_rows = (hg * swished).astype(BF)
    for k in range(2):
        half = slice(k * N // 2, (k + 1) * N // 2)
        R[y, k, 0] = gate_rows[half]
        R[y, k, 1] = up_rows[half]
        R[y, k, 2] = hidden[half]

    ys, yr = ysems
    y_half = Y // 2

    def y_forward(held, units):
        for k in (held + 2, held + 1):
            if k <= y_half:
                for way in range(2):
                    step = k - held if way == 0 else Y - (k - held)
                    to = device(lax.rem(y + step, Y), z, c, x)
                    part = R.at[units[way]] if k < y_half else R.at[units[way], way]
                    go(remote(part, part, ys.at[way, k], yr.at[way, k], to))

    def y_arrive(k):
        units = (lax.rem(y + Y - k, Y), lax.rem(y + k, Y))
        for way in range(2):
            part = R.at[units[way]] if k < y_half else R.at[units[way], way]
            remote(part, part, ys.at[way, k], yr.at[way, k], device(y, z, c, x)).wait_recv()
        if k % 2 == 0:
            y_forward(k, units)

    y_order = [k for pair in tree(y_half) for k in pair]
    y_forward(0, (y, y))

    todo = wide.events()

    def wide_events(n):
        for _ in range(min(n, len(todo))):
            todo.pop(0)()

    wide_events(2)

    f_as, f_ar, f_bs, f_br, f_cs, f_cr, f_ds, f_dr = fsems
    B[...] = jnp.concatenate([gate_rows, up_rows], axis=1).reshape(Z, 16, 2 * ff)
    order = farthest_first(Z)
    both = jnp.concatenate([B[lax.rem(z + d, Z)] for d in order], axis=0)
    other = device(y, z, 1 - c, x)
    x_order = farthest_first(X)

    def columns(cc, xx):
        at = pl.multiple_of((cc * X + xx) * CW, CW)
        return dot(both, wgu[pl.ds(at, CW), :], 1, 1)

    for d in x_order:
        FAs[d] = columns(1 - c, lax.rem(x + d, X)).astype(BF)
        go(remote(FAs.at[d], FAr.at[d], f_as.at[d], f_ar.at[d], other))
    wide_events(1)
    Zh = Z // 2

    def across(d, g):
        return FBs.at[d, g], FBr.at[d, g], f_bs.at[d, g], f_br.at[d, g]

    for d in x_order:
        xx = lax.rem(x + d, X)
        summed = columns(c, xx)
        remote(FAs.at[d], FAr.at[d], f_as.at[d], f_ar.at[d], other).wait_recv()
        summed += FAr[d].astype(F32)
        if d:
            FBs[d] = summed.reshape(2, Zh, 16, CW).astype(BF)
            go(remote(*across(d, 0), device(y, z, c, xx)))
        else:
            FT[...] = summed.reshape(Z, 16, CW)
    for d in x_order[:-1]:
        go(remote(*across(d, 1), device(y, z, c, lax.rem(x + d, X))))
    wide_events(4)
    for g in range(2):
        total = FT[g * Zh : (g + 1) * Zh]
        for d in x_order[:-1]:
            remote(*across(d, g), other).wait_recv()
            total += FBr[d, g].astype(F32)
        FCs[g * Zh : (g + 1) * Zh] = total.astype(BF)
        for k in range(g * Zh, (g + 1) * Zh):
            d = order[k]
            if d:
                to = device(y, lax.rem(z + d, Z), c, x)
                go(remote(FCs.at[k], FCr.at[d], f_cs.at[d], f_cr.at[d], to))
        if g == 1:
            FT[0] = total[Zh - 1]
        wide_events(2)
    y_arrive(y_order[0])
    wide_events(len(todo))
    for k in y_order[1:2]:
        y_arrive(k)
    total = FT[0]
    for d in range(1, Z):
        remote(FCs.at[0], FCr.at[d], f_cs.at[d], f_cr.at[d], other).wait_recv()
        total += FCr[d].astype(F32)
    FDr[mine] = total.astype(BF)
    for d in range(1, 2 * X):
        go(remote(FDr.at[mine], FDr.at[mine], f_ds.at[d], f_dr.at[d], corner(d)))
    wide.finish()

    def accumulate(unit, first):
        rows_g = jnp.concatenate([R[unit, 0, 0], R[unit, 1, 0]], axis=0)
        rows_u = jnp.concatenate([R[unit, 0, 1], R[unit, 1, 1]], axis=0)
        rows_h = jnp.concatenate([R[unit, 0, 2], R[unit, 1, 2]], axis=0)
        gu_rows = jnp.concatenate([rows_g, rows_u], axis=1)
        for h in range(2):
            for q in range(2):
                at = (h * 2 + q) * HD
                a = H[:, :, h, q, unit].astype(F32).reshape(Z * 2, 2, SLOTS, HD)
                nrm = a[:, 0].reshape(N, HD).astype(BF)
                msk = a[:, 1].reshape(N, HD).astype(BF)
                pair = dot(nrm, gu_rows, 0, 0)
                down = dot(rows_h, msk, 0, 0)
                if first:
                    out_g[at : at + HD, :] = pair[:, :ff]
                    out_u[at : at + HD, :] = pair[:, ff:]
                    out_d[:, at : at + HD] = down
                else:
                    out_g[at : at + HD, :] += pair[:, :ff]
                    out_u[at : at + HD, :] += pair[:, ff:]
                    out_d[:, at : at + HD] += down

    def accumulate_pair(k):
        accumulate(lax.rem(y + Y - k, Y), False)
        if k < y_half:
            accumulate(lax.rem(y + k, Y), False)

    accumulate(y, True)
    for k in y_order[:2]:
        if k < y_half:
            accumulate_pair(k)

    for d in range(1, 2 * X):
        j = lax.rem(mine + 2 * X - d, 2 * X)
        remote(FDr.at[j], FDr.at[j], f_ds.at[d], f_dr.at[d], other).wait_recv()
    pieces = []
    for j in range(2 * X):
        piece = FDr[j].astype(F32)
        pieces.append(jnp.where(c == 0, piece[:SLOTS], piece[SLOTS:]))
    feature = jnp.concatenate(pieces, axis=1)
    src = source[...]
    scale = lax.rsqrt(jnp.mean(src * src, axis=-1, keepdims=True) + EPSILON)
    weighted = feature * gain_ref[...]
    along = jnp.mean(weighted * src, axis=-1, keepdims=True)
    grad = weighted * scale - src * (scale * scale * scale * along)
    out_s[...] = jnp.concatenate([grad, jnp.zeros_like(grad)], axis=0).astype(BF)

    for k in y_order[2:]:
        y_arrive(k)
    for k in y_order:
        if k in y_order[2:] or k == y_half:
            accumulate_pair(k)
    for copy in sent:
        copy.wait_send()


def results(slots, picks, g_in, u_in, d_in, branch, g_out, u_out, d_out):
    branch[...] = dot(picks[...], slots[...]).astype(BF)
    g_out[...] = g_in[...]
    u_out[...] = u_in[...]
    d_out[...] = d_in[...]


def local(sizes, tokens, cotangent, norm_gain, gate_weight, up_weight, down_weight, depths):
    Y, Z, X = sizes
    n_tok, D = tokens.shape
    ff = gate_weight.shape[1]
    N = Z * 2 * SLOTS
    QD, HD, CW = D // 4, D // (4 * Y), D // (2 * X)
    vmem, dma = pltpu.VMEM, pltpu.SemaphoreType.DMA
    steps = Z // 2 + 1
    plane = (
        dma((2, steps)),
        dma((2, steps)),
        dma((2, steps, 2)),
        dma((2, steps, 2)),
        dma((2, steps, 2)),
        dma((2, steps, 2)),
    )
    hbm, whole = pl.BlockSpec(memory_space=pl.ANY), pl.BlockSpec(memory_space=pltpu.VMEM)
    grads = (
        jax.ShapeDtypeStruct((D // Y, ff), F32),
        jax.ShapeDtypeStruct((D // Y, ff), F32),
        jax.ShapeDtypeStruct((ff, D // Y), F32),
    )
    parts = pl.pallas_call(
        functools.partial(kernel, sizes),
        out_shape=(
            jax.ShapeDtypeStruct((16, D), BF),
            jax.ShapeDtypeStruct((n_tok // X, 16), BF),
            *grads,
        ),
        in_specs=[hbm, hbm, whole, hbm, hbm, hbm, whole],
        out_specs=(whole,) * 5,
        scratch_shapes=[
            vmem((n_tok, D), BF),
            vmem((n_tok, D), BF),
            vmem((D, 2 * ff), BF),
            vmem((ff, D), BF),
            vmem((SLOTS, D), F32),
            vmem((Z, 2, 2, 2, 16, QD), BF),
            vmem((Z, 2, 2, 2, Y, 16, HD), BF),
            vmem((Y, 2, 2, 16, HD), BF),
            vmem((Y, 2, 3, N // 2, ff), BF),
            vmem((X, N, CW), BF),
            vmem((X, N, CW), BF),
            vmem((Z, 16, 2 * ff), BF),
            vmem((X, 2, Z // 2, 16, CW), BF),
            vmem((X, 2, Z // 2, 16, CW), BF),
            vmem((Z, 16, CW), F32),
            vmem((Z, 16, CW), BF),
            vmem((Z, 16, CW), BF),
            vmem((2 * X, 16, CW), BF),
            dma((5,)),
            plane,
            plane,
            (dma((Y,)), dma((Y,))),
            (dma((2, Y // 2 + 1)), dma((2, Y // 2 + 1))),
            (
                dma((X,)),
                dma((X,)),
                dma((X, 2)),
                dma((X, 2)),
                dma((Z,)),
                dma((Z,)),
                dma((2 * X,)),
                dma((2 * X,)),
            ),
        ],
        compiler_params=pltpu.CompilerParams(
            collective_id=0, has_side_effects=True, vmem_limit_bytes=58 * 1024 * 1024
        ),
    )(
        tokens,
        cotangent,
        norm_gain.reshape(1, D),
        gate_weight,
        up_weight,
        down_weight,
        depths.reshape(1, n_tok),
    )
    return pl.pallas_call(
        results,
        out_shape=(jax.ShapeDtypeStruct((n_tok // X, D), BF), *grads),
        in_specs=[whole] * 5,
        out_specs=(whole,) * 4,
    )(*parts)


def solution(mesh):
    sizes = (mesh.shape["rep"], mesh.shape["seq"] // 2, mesh.shape["fsdp"])
    rows, hidden = ("rep", "seq"), ("seq", "fsdp")
    return jax.shard_map(
        functools.partial(local, sizes),
        mesh=mesh,
        in_specs=(
            P(rows, None),
            P(rows, None),
            P(),
            P(None, hidden),
            P(None, hidden),
            P(hidden, None),
            P(rows),
        ),
        out_specs=(
            P(("rep", "seq", "fsdp"), None),
            P("rep", hidden),
            P("rep", hidden),
            P(hidden, "rep"),
        ),
        check_vma=False,
    )
```

```python
import functools

import jax
import jax.numpy as jnp
from jax import lax
from jax.experimental import pallas as pl
from jax.experimental.pallas import tpu as pltpu
from jax.sharding import PartitionSpec as P

REC = 1
SLOTS = 8
EPSILON = 1e-05
MESH = pl.DeviceIdType.MESH
BF = jnp.bfloat16
F32 = jnp.float32


def dot(a, b, da=1, db=0):
    return lax.dot_general(a, b, (((da,), (db,)), ((), ())), preferred_element_type=F32)


def remote(src, dst, ssem, rsem, device):
    return pltpu.make_async_remote_copy(
        src_ref=src,
        dst_ref=dst,
        send_sem=ssem,
        recv_sem=rsem,
        device_id=device,
        device_id_type=MESH,
    )


def tree(half):
    return [[s for s in (g + 2, g + 1) if s <= half] for g in range(0, half, 2)]


def farthest_first(n):
    return sorted(range(n), key=lambda d: -min(d, n - d))


class PlaneGather:
    def __init__(self, buf, sems, where, sizes, device, sent):
        self.buf, self.sent, self.device = buf, sent, device
        self.zs, self.zr, self.xs, self.xr, self.cs, self.cr = sems
        self.y, self.z, self.c, self.x = where
        self.Y, self.Z, self.X = sizes
        self.p = lax.rem(self.x, 2)
        self.half = self.Z // 2
        self.here = device(self.y, self.z, self.c, self.x)
        self.groups = tree(self.half)

    def events(self):
        found = []
        self.last_forward = None
        for k, group in enumerate(self.groups):
            found.append(functools.partial(self.arrive, group[0]))
            if k + 1 < len(self.groups):
                self.last_forward = found[-1]
            if k:
                found += [functools.partial(self.beside, s) for s in self.groups[k - 1]]
            found += [functools.partial(self.arrive, s) for s in group[1:]]
        return found + [functools.partial(self.beside, s) for s in self.groups[-1]]

    def zz(self, way, s):
        return lax.rem(self.z + (self.Z - s if way == 0 else s), self.Z)

    def go(self, copy):
        copy.start()
        self.sent.append(copy)

    def quarters(self, way, s):
        return (0, 1) if s < self.half else (way,)

    def part(self, way, s, block, c, h):
        whole = self.buf.at[block, c, h]
        return whole if s < self.half else self.buf.at[block, c, h, way]

    def forward(self, held, block):
        for s in (held + 2, held + 1):
            if s <= self.half:
                for way in range(2):
                    step = s - held if way == 0 else self.Z - (s - held)
                    to = self.device(self.y, lax.rem(self.z + step, self.Z), self.c, self.x)
                    part = self.part(way, s, block[way], self.c, self.p)
                    self.go(remote(part, part, self.zs.at[way, s], self.zr.at[way, s], to))

    def to_core(self, part, way, s, kind):
        to = self.device(self.y, self.z, 1 - self.c, self.x)
        self.go(remote(part, part, self.cs.at[way, s, kind], self.cr.at[way, s, kind], to))

    def start(self):
        self.forward(0, (self.z, self.z))
        self.to_core(self.buf.at[self.z, self.c], 0, 0, 0)

    def arrive(self, s):
        blocks = (self.zz(0, s), self.zz(1, s))
        parts = [self.part(way, s, blocks[way], self.c, self.p) for way in range(2)]
        for way in range(2):
            remote(
                parts[way], parts[way], self.zs.at[way, s], self.zr.at[way, s], self.here
            ).wait_recv()
        if s % 2 == 0:
            self.forward(s, blocks)
        for way in range(2):
            for q in self.quarters(way, s):
                xx = lax.rem(self.x + (1 if q == 0 else self.X - 1), self.X)
                to = self.device(self.y, self.z, self.c, xx)
                quarter = self.buf.at[blocks[way], self.c, self.p, q]
                self.go(
                    remote(quarter, quarter, self.xs.at[way, s, q], self.xr.at[way, s, q], to)
                )
            self.to_core(parts[way], way, s, 0)

    def beside(self, s):
        for way in range(2):
            block = self.zz(way, s)
            for q in self.quarters(way, s):
                quarter = self.buf.at[block, self.c, 1 - self.p, q]
                remote(
                    quarter, quarter, self.xs.at[way, s, q], self.xr.at[way, s, q], self.here
                ).wait_recv()
            self.to_core(self.part(way, s, block, self.c, 1 - self.p), way, s, 1)

    def finish(self):
        part = self.buf.at[self.z, 1 - self.c]
        remote(part, part, self.cs.at[0, 0, 0], self.cr.at[0, 0, 0], self.here).wait_recv()
        for s in range(1, self.half + 1):
            for way in range(2):
                block = self.zz(way, s)
                for kind in range(2):
                    h = self.p if kind == 0 else 1 - self.p
                    part = self.part(way, s, block, 1 - self.c, h)
                    remote(
                        part, part, self.cs.at[way, s, kind], self.cr.at[way, s, kind], self.here
                    ).wait_recv()


def kernel(
    sizes,
    tok_hbm,
    cot_hbm,
    gain_ref,
    gw_hbm,
    uw_hbm,
    dw_hbm,
    dep_ref,
    out_s,
    out_p,
    out_g,
    out_u,
    out_d,
    tok,
    cot,
    wgu,
    dw,
    source,
    G,
    H,
    S,
    R,
    FAs,
    FAr,
    B,
    FBs,
    FBr,
    FT,
    FCs,
    FCr,
    FDr,
    lsem,
    gsems,
    hsems,
    asems,
    ysems,
    fsems,
):
    Y, Z, X = sizes
    n_tok, D = tok.shape
    ff = dw.shape[0]
    N = Z * 2 * SLOTS
    QD, HD, CW = D // 4, D // (4 * Y), D // (2 * X)
    y, x = lax.axis_index("rep"), lax.axis_index("fsdp")
    seq = lax.axis_index("seq")
    z, c = seq // 2, lax.rem(seq, 2)

    def device(yy, zz, cc, xx):
        return (yy, zz * 2 + cc, xx)

    loads = [
        pltpu.make_async_copy(tok_hbm, tok, lsem.at[0]),
        pltpu.make_async_copy(cot_hbm, cot, lsem.at[1]),
        pltpu.make_async_copy(gw_hbm, wgu.at[:, 0:ff], lsem.at[2]),
        pltpu.make_async_copy(uw_hbm, wgu.at[:, ff : 2 * ff], lsem.at[3]),
        pltpu.make_async_copy(dw_hbm, dw, lsem.at[4]),
    ]
    for load in loads:
        load.start()

    partners = [device(lax.rem(y + d, Y), z, c, x) for d in range(1, Y)]
    partners += [device(y, lax.rem(z + d, Z), c, x) for d in range(1, Z)]
    mine = c * X + x

    def corner(d):
        j = lax.rem(mine + d, 2 * X)
        return device(y, z, j // X, lax.rem(j, X))

    partners += [corner(d) for d in range(1, 2 * X)]
    barrier = pltpu.get_barrier_semaphore()
    for partner in partners:
        pl.semaphore_signal(barrier, inc=1, device_id=partner, device_id_type=MESH)

    act = jnp.where(dep_ref[...] > REC, 1.0, 0.0).astype(F32)
    act = jnp.broadcast_to(act, (16, n_tok))
    before = lax.broadcasted_iota(jnp.int32, (n_tok, n_tok), 0)
    after = lax.broadcasted_iota(jnp.int32, (n_tok, n_tok), 1)
    tri = jnp.where(before <= after, 1.0, 0.0).astype(BF)
    ordinal = dot(act.astype(BF), tri) - 1.0
    slot = lax.broadcasted_iota(jnp.int32, (16, n_tok), 0).astype(F32)
    sel = jnp.where((ordinal == slot) & (act > 0.5), 1.0, 0.0).astype(BF)
    own = n_tok // X
    i0 = lax.broadcasted_iota(jnp.int32, (own, n_tok), 0)
    i1 = lax.broadcasted_iota(jnp.int32, (own, n_tok), 1)
    rows = jnp.where(i1 == i0 + x * own, 1.0, 0.0).astype(BF)
    out_p[...] = dot(rows, sel, 1, 1).astype(BF)
    loads[0].wait()
    tsel = dot(sel, tok[...])
    factor = lax.rsqrt(jnp.mean(tsel * tsel, axis=-1, keepdims=True) + EPSILON)
    normed = tsel * factor * gain_ref[...]
    source[...] = tsel[:SLOTS]
    loads[1].wait()
    csel = dot(sel, cot[...])
    block = jnp.concatenate([normed[:SLOTS], csel[:SLOTS]], axis=0).astype(BF)
    for h in range(2):
        for q in range(2):
            at = (h * 2 + q) * QD
            G[z, c, h, q] = block[:, at : at + QD]
    for yy in range(Y):
        for h in range(2):
            for q in range(2):
                at = (yy * 4 + h * 2 + q) * HD
                S[yy, h, q] = block[:, at : at + HD]

    pl.semaphore_wait(barrier, len(partners))

    sent = []

    def go(copy):
        copy.start()
        sent.append(copy)

    where = (y, z, c, x)
    gather = PlaneGather(G, gsems, where, sizes, device, sent)
    gather.start()
    as_, ar = asems
    for d in range(1, Y):
        yy = lax.rem(y + d, Y)
        go(
            remote(
                S.at[yy], H.at[z, c, :, :, Y - 1 - d], as_.at[d], ar.at[d], device(yy, z, c, x)
            )
        )
    wide = PlaneGather(H, hsems, where, sizes, device, sent)
    events = gather.events()
    behind = events.index(gather.last_forward) + 1 if gather.last_forward else 0
    for event in events[:behind]:
        event()
    for d in range(1, Y):
        part = H.at[z, c, :, :, Y - 1 - d]
        remote(S.at[y], part, as_.at[d], ar.at[d], device(y, z, c, x)).wait_recv()
    wide.start()
    for event in events[behind:]:
        event()
    gather.finish()
    todo = wide.events()

    def wide_events(n):
        for _ in range(min(n, len(todo))):
            todo.pop(0)()

    wide_events(1)

    for load in loads[2:]:
        load.wait()
    gu = jnp.zeros((2 * N, 2 * ff), F32)
    hd = jnp.zeros((2 * N, ff), F32)
    for h in range(2):
        for q in range(2):
            at = (h * 2 + q) * QD
            a = G[:, :, h, q].reshape(2 * N, QD)
            gu += dot(a, wgu[at : at + QD, :])
            hd += dot(a, dw[:, at : at + QD], 1, 1)
    gu = gu.reshape(Z * 2, 2, SLOTS, 2 * ff)[:, 0].reshape(N, 2 * ff)
    hg = hd.reshape(Z * 2, 2, SLOTS, ff)[:, 1].reshape(N, ff)
    gate, up = gu[:, :ff], gu[:, ff:]
    sig = jax.nn.sigmoid(gate)
    swished = gate * sig
    hidden = (swished * up).astype(BF)
    gate_rows = (hg * up * sig * (1.0 + gate * (1.0 - sig))).astype(BF)
    up_rows = (hg * swished).astype(BF)
    for k in range(2):
        half = slice(k * N // 2, (k + 1) * N // 2)
        R[y, k, 0] = gate_rows[half]
        R[y, k, 1] = up_rows[half]
        R[y, k, 2] = hidden[half]

    ys, yr = ysems
    y_half = Y // 2

    def y_forward(held, units):
        for k in (held + 2, held + 1):
            if k <= y_half:
                for way in range(2):
                    step = k - held if way == 0 else Y - (k - held)
                    to = device(lax.rem(y + step, Y), z, c, x)
                    part = R.at[units[way]] if k < y_half else R.at[units[way], way]
                    go(remote(part, part, ys.at[way, k], yr.at[way, k], to))

    def y_arrive(k):
        units = (lax.rem(y + Y - k, Y), lax.rem(y + k, Y))
        for way in range(2):
            part = R.at[units[way]] if k < y_half else R.at[units[way], way]
            remote(part, part, ys.at[way, k], yr.at[way, k], device(y, z, c, x)).wait_recv()
        if k % 2 == 0:
            y_forward(k, units)

    y_order = [k for pair in tree(y_half) for k in pair]
    y_forward(0, (y, y))

    wide_events(1)

    f_as, f_ar, f_bs, f_br, f_cs, f_cr, f_ds, f_dr = fsems
    B[...] = jnp.concatenate([gate_rows, up_rows], axis=1).reshape(Z, 16, 2 * ff)
    order = farthest_first(Z)
    both = jnp.concatenate([B[lax.rem(z + d, Z)] for d in order], axis=0)
    other = device(y, z, 1 - c, x)
    x_order = farthest_first(X)

    def columns(cc, xx):
        at = pl.multiple_of((cc * X + xx) * CW, CW)
        return dot(both, wgu[pl.ds(at, CW), :], 1, 1)

    for d in x_order:
        FAs[d] = columns(1 - c, lax.rem(x + d, X)).astype(BF)
        go(remote(FAs.at[d], FAr.at[d], f_as.at[d], f_ar.at[d], other))
    wide_events(1)
    Zh = Z // 2

    def across(d, g):
        return FBs.at[d, g], FBr.at[d, g], f_bs.at[d, g], f_br.at[d, g]

    for d in x_order:
        xx = lax.rem(x + d, X)
        summed = columns(c, xx)
        remote(FAs.at[d], FAr.at[d], f_as.at[d], f_ar.at[d], other).wait_recv()
        summed += FAr[d].astype(F32)
        if d:
            FBs[d] = summed.reshape(2, Zh, 16, CW).astype(BF)
            go(remote(*across(d, 0), device(y, z, c, xx)))
        else:
            FT[...] = summed.reshape(Z, 16, CW)
    for d in x_order[:-1]:
        go(remote(*across(d, 1), device(y, z, c, lax.rem(x + d, X))))
    wide_events(3)
    for g in range(2):
        total = FT[g * Zh : (g + 1) * Zh]
        for d in x_order[:-1]:
            remote(*across(d, g), other).wait_recv()
            total += FBr[d, g].astype(F32)
        FCs[g * Zh : (g + 1) * Zh] = total.astype(BF)
        for k in range(g * Zh, (g + 1) * Zh):
            d = order[k]
            if d:
                to = device(y, lax.rem(z + d, Z), c, x)
                go(remote(FCs.at[k], FCr.at[d], f_cs.at[d], f_cr.at[d], to))
        if g == 1:
            FT[0] = total[Zh - 1]
        wide_events((1, 3)[g])
    y_arrive(y_order[0])
    for k in y_order[1:2]:
        y_arrive(k)
    total = FT[0]
    for d in range(1, Z):
        remote(FCs.at[0], FCr.at[d], f_cs.at[d], f_cr.at[d], other).wait_recv()
        total += FCr[d].astype(F32)
    FDr[mine] = total.astype(BF)
    for d in range(1, 2 * X):
        go(remote(FDr.at[mine], FDr.at[mine], f_ds.at[d], f_dr.at[d], corner(d)))

    at_own = y * (4 * HD)
    own_h, own_q = at_own // (2 * QD), lax.rem(at_own // QD, 2)

    def block_of(slot, h, q):
        if slot is not None:
            return H[:, :, h, q, slot]
        at = pl.multiple_of(lax.rem(at_own, QD) + (h * 2 + q) * HD, HD)
        return G[:, :, own_h, own_q, :, pl.ds(at, HD)]

    def accumulate(unit, slot=None):
        rows_g = jnp.concatenate([R[unit, 0, 0], R[unit, 1, 0]], axis=0)
        rows_u = jnp.concatenate([R[unit, 0, 1], R[unit, 1, 1]], axis=0)
        rows_h = jnp.concatenate([R[unit, 0, 2], R[unit, 1, 2]], axis=0)
        gu_rows = jnp.concatenate([rows_g, rows_u], axis=1)
        for h in range(2):
            for q in range(2):
                at = (h * 2 + q) * HD
                a = block_of(slot, h, q).astype(F32).reshape(Z * 2, 2, SLOTS, HD)
                nrm = a[:, 0].reshape(N, HD).astype(BF)
                msk = a[:, 1].reshape(N, HD).astype(BF)
                pair = dot(nrm, gu_rows, 0, 0)
                down = dot(rows_h, msk, 0, 0)
                if slot is None:
                    out_g[at : at + HD, :] = pair[:, :ff]
                    out_u[at : at + HD, :] = pair[:, ff:]
                    out_d[:, at : at + HD] = down
                else:
                    out_g[at : at + HD, :] += pair[:, :ff]
                    out_u[at : at + HD, :] += pair[:, ff:]
                    out_d[:, at : at + HD] += down

    def accumulate_pair(k):
        accumulate(lax.rem(y + Y - k, Y), Y - 1 - k)
        if k < y_half:
            accumulate(lax.rem(y + k, Y), k - 1)

    wide_events(len(todo))
    wide.finish()
    accumulate(y)
    for k in y_order[:2]:
        if k < y_half:
            accumulate_pair(k)

    for d in range(1, 2 * X):
        j = lax.rem(mine + 2 * X - d, 2 * X)
        remote(FDr.at[j], FDr.at[j], f_ds.at[d], f_dr.at[d], other).wait_recv()
    pieces = []
    for j in range(2 * X):
        piece = FDr[j].astype(F32)
        pieces.append(jnp.where(c == 0, piece[:SLOTS], piece[SLOTS:]))
    feature = jnp.concatenate(pieces, axis=1)
    src = source[...]
    scale = lax.rsqrt(jnp.mean(src * src, axis=-1, keepdims=True) + EPSILON)
    weighted = feature * gain_ref[...]
    along = jnp.mean(weighted * src, axis=-1, keepdims=True)
    grad = weighted * scale - src * (scale * scale * scale * along)
    out_s[...] = jnp.concatenate([grad, jnp.zeros_like(grad)], axis=0).astype(BF)

    for k in y_order[2:]:
        y_arrive(k)
    for k in y_order:
        if k in y_order[2:] or k == y_half:
            accumulate_pair(k)
    for copy in sent:
        copy.wait_send()


def results(slots, picks, g_in, u_in, d_in, branch, g_out, u_out, d_out):
    branch[...] = dot(picks[...], slots[...]).astype(BF)
    g_out[...] = g_in[...]
    u_out[...] = u_in[...]
    d_out[...] = d_in[...]


def local(sizes, tokens, cotangent, norm_gain, gate_weight, up_weight, down_weight, depths):
    Y, Z, X = sizes
    n_tok, D = tokens.shape
    ff = gate_weight.shape[1]
    N = Z * 2 * SLOTS
    QD, HD, CW = D // 4, D // (4 * Y), D // (2 * X)
    vmem, dma = pltpu.VMEM, pltpu.SemaphoreType.DMA
    steps = Z // 2 + 1
    plane = (
        dma((2, steps)),
        dma((2, steps)),
        dma((2, steps, 2)),
        dma((2, steps, 2)),
        dma((2, steps, 2)),
        dma((2, steps, 2)),
    )
    hbm, whole = pl.BlockSpec(memory_space=pl.ANY), pl.BlockSpec(memory_space=pltpu.VMEM)
    grads = (
        jax.ShapeDtypeStruct((D // Y, ff), F32),
        jax.ShapeDtypeStruct((D // Y, ff), F32),
        jax.ShapeDtypeStruct((ff, D // Y), F32),
    )
    parts = pl.pallas_call(
        functools.partial(kernel, sizes),
        out_shape=(
            jax.ShapeDtypeStruct((16, D), BF),
            jax.ShapeDtypeStruct((n_tok // X, 16), BF),
            *grads,
        ),
        in_specs=[hbm, hbm, whole, hbm, hbm, hbm, whole],
        out_specs=(whole,) * 5,
        scratch_shapes=[
            vmem((n_tok, D), BF),
            vmem((n_tok, D), BF),
            vmem((D, 2 * ff), BF),
            vmem((ff, D), BF),
            vmem((SLOTS, D), F32),
            vmem((Z, 2, 2, 2, 16, QD), BF),
            vmem((Z, 2, 2, 2, Y - 1, 16, HD), BF),
            vmem((Y, 2, 2, 16, HD), BF),
            vmem((Y, 2, 3, N // 2, ff), BF),
            vmem((X, N, CW), BF),
            vmem((X, N, CW), BF),
            vmem((Z, 16, 2 * ff), BF),
            vmem((X, 2, Z // 2, 16, CW), BF),
            vmem((X, 2, Z // 2, 16, CW), BF),
            vmem((Z, 16, CW), F32),
            vmem((Z, 16, CW), BF),
            vmem((Z, 16, CW), BF),
            vmem((2 * X, 16, CW), BF),
            dma((5,)),
            plane,
            plane,
            (dma((Y,)), dma((Y,))),
            (dma((2, Y // 2 + 1)), dma((2, Y // 2 + 1))),
            (
                dma((X,)),
                dma((X,)),
                dma((X, 2)),
                dma((X, 2)),
                dma((Z,)),
                dma((Z,)),
                dma((2 * X,)),
                dma((2 * X,)),
            ),
        ],
        compiler_params=pltpu.CompilerParams(
            collective_id=0, has_side_effects=True, vmem_limit_bytes=58 * 1024 * 1024
        ),
    )(
        tokens,
        cotangent,
        norm_gain.reshape(1, D),
        gate_weight,
        up_weight,
        down_weight,
        depths.reshape(1, n_tok),
    )
    return pl.pallas_call(
        results,
        out_shape=(jax.ShapeDtypeStruct((n_tok // X, D), BF), *grads),
        in_specs=[whole] * 5,
        out_specs=(whole,) * 4,
    )(*parts)


def solution(mesh):
    sizes = (mesh.shape["rep"], mesh.shape["seq"] // 2, mesh.shape["fsdp"])
    rows, hidden = ("rep", "seq"), ("seq", "fsdp")
    return jax.shard_map(
        functools.partial(local, sizes),
        mesh=mesh,
        in_specs=(
            P(rows, None),
            P(rows, None),
            P(),
            P(None, hidden),
            P(None, hidden),
            P(hidden, None),
            P(rows),
        ),
        out_specs=(
            P(("rep", "seq", "fsdp"), None),
            P("rep", hidden),
            P("rep", hidden),
            P(hidden, "rep"),
        ),
        check_vma=False,
    )
```
